32 devices in a mesh: dp: 4 (over y, core), expert: 8 (over z, x).
Axes of the slice: x: 2, y: 2, z: 4, core: 2. Of those that a mesh axis runs over, the one named last changes fastest.
Arguments:
- x_in: bfloat16 [4096, 1024], P(('dp', 'expert')), may hold values from -6 to 6
- grad_out: bfloat16 [4096, 1024], P(('dp', 'expert')), may hold values from -6 to 6
- routes: int32 [4096, 8], P(('dp', 'expert')), may hold values from 0 to 7, as said below
- gate_probs: float32 [4096, 8], P(('dp', 'expert')), may hold values from 0.05 to 1
- gate_up: bfloat16 [8, 1024, 768], P('expert'), may hold values from -0.1875 to 0.1875
- down: bfloat16 [8, 1024, 384], P('expert'), may hold values from -0.3125 to 0.3125
Outputs:
- grad_in: bfloat16 [4096, 1024], P(('dp', 'expert'))
- grad_gate_up: float32 [8, 1024, 768], P('expert', 'dp')
- grad_down: float32 [8, 1024, 384], P('expert', 'dp')
The draws below stay inside these ranges and needn't reach their ends.
Inputs may be any that keep to these rules, and one draw needn't show every extreme that they name: `routes`: each row names 8 different experts. Among the rows of one device no expert is named more than 128 times, and on every device some expert is named exactly 128 times.
All inputs are finite; a program needn't handle non-finite values.
Results may differ from the reference program's by a relative error of at most 0.02.
Values may be sent and summed in bfloat16 or wider, within the bound.
A program may use at most 64 MiB of HBM per device.

```python
import math
import jax
import jax.numpy as jnp
from jax import lax

D = 1024
FF = 384
TOP = 8
TOK_DEV = 128
EXPERTS = 8
CAP = 128
TOKENS = 4096
N_DP = 4
N_EXPERT = 8


def draw_routes(key, part):
    block_count = TOKENS // TOK_DEV
    hot_expert = jax.random.randint(jax.random.fold_in(key, 7), (), 0, EXPERTS).astype(jnp.int32)

    def one_block(block_key):
        key_one, key_two, key_three, key_four = jax.random.split(block_key, 4)
        labels = jnp.arange(EXPERTS, dtype=jnp.int32)
        is_hot = labels == hot_expert
        weights = jnp.where(is_hot, 0, jax.random.randint(key_one, (EXPERTS,), 1, 8).astype(jnp.int32))
        deficit = EXPERTS * CAP - TOK_DEV * TOP
        share = weights * deficit // jnp.sum(weights)
        leftover = deficit - jnp.sum(share)
        order = jax.random.permutation(key_two, EXPERTS).astype(jnp.int32)
        hot_order = jnp.sum(jnp.where(is_hot, order, 0))
        position = jnp.where(is_hot, EXPERTS, order - (order > hot_order).astype(jnp.int32))
        share = share + (position < leftover).astype(jnp.int32)
        loads = jnp.where(is_hot, CAP, CAP - share).astype(jnp.int32)
        label_order = jax.random.permutation(key_three, EXPERTS).astype(jnp.int32)
        ordered = loads[label_order]
        ends = jnp.cumsum(ordered)
        entry_ids = jnp.arange(TOK_DEV * TOP, dtype=jnp.int32)
        which = jnp.sum((ends[None, :] <= entry_ids[:, None]).astype(jnp.int32), axis=1)
        flat_ids = label_order[which]
        table_rows = flat_ids.reshape(TOP, TOK_DEV).T
        shuffle = jax.random.permutation(key_four, TOK_DEV)
        return table_rows[shuffle]
    block_keys = jax.vmap(lambda index: jax.random.fold_in(key, index + 11))(jnp.arange(block_count, dtype=jnp.int32))
    return jax.vmap(one_block)(block_keys).reshape(TOKENS, TOP).astype(jnp.int32)


def shard_levels(stream_key, dims, cuts, least, high):
    gain, own = 1.0, jax.random.fold_in(stream_key, 6)
    for dim, blocks in cuts:
        heights = jnp.exp(jax.random.uniform(jax.random.fold_in(own, dim), (blocks,), jnp.float32, least / len(cuts), high / len(cuts)))
        gain = gain * jnp.repeat(heights, dims[dim] // blocks).reshape([-1 if axis == dim else 1 for axis in range(len(dims))])
    return gain


def scatter_about(stream_key, dims, deviation, bound, shards=(), held_as=jnp.bfloat16):
    values = deviation * jax.random.normal(stream_key, dims, jnp.float32)
    if shards:
        values = values * shard_levels(stream_key, dims, shards, -0.22, 0.18)
    return jnp.clip(values, -bound, bound).astype(held_as)


def setup_inputs(seed: int = 0) -> dict:
    key_list = jax.random.split(jax.random.key(seed), 7)
    x_in = scatter_about(key_list[0], (TOKENS, D), 1.0, 6.0, ((0, 32),))
    grad_out = scatter_about(key_list[1], (TOKENS, D), 1.0, 6.0, ((0, 32),))
    routes = draw_routes(jax.random.fold_in(key_list[6], 71), 0)
    gate_probs = jnp.clip(jnp.exp(math.log(1.0) - 2.9957323 * jax.random.uniform(key_list[3], (TOKENS, TOP), jnp.float32) ** shard_levels(key_list[3], (TOKENS, TOP), ((0, 32),), -0.2, 0.2)), 0.05, 1.0)
    gate_up = scatter_about(key_list[4], (EXPERTS, D, 2 * FF), D ** -0.5, 0.1875, ((0, 8),))
    down = scatter_about(key_list[5], (EXPERTS, D, FF), FF ** -0.5, 0.3125, ((0, 8),))
    return dict(x_in=x_in, grad_out=grad_out, routes=routes, gate_probs=gate_probs, gate_up=gate_up, down=down)


def slot_ranks(flat_ids):
    onehot = (flat_ids[:, None] == jnp.arange(EXPERTS, dtype=jnp.int32)[None, :]).astype(jnp.int32)
    before = jnp.cumsum(onehot, axis=0) - onehot
    return jnp.sum(before * onehot, axis=1).astype(jnp.int32)


def dispatch_table(route_block):
    flat_ids = route_block.reshape(-1).astype(jnp.int32)
    count_rows = flat_ids.shape[0]
    slot_rank = slot_ranks(flat_ids)
    entry_pos = (flat_ids * CAP + slot_rank).astype(jnp.int32)
    slot_table = jnp.full((EXPERTS * CAP,), count_rows, jnp.int32)
    slot_table = slot_table.at[entry_pos].set(jnp.arange(count_rows, dtype=jnp.int32))
    return slot_table, entry_pos


def send_rows(x_block, grad_block, prob_block, slot_table):
    token_pos = (slot_table // TOP).astype(jnp.int32)
    x_padded = jnp.concatenate([x_block, jnp.zeros((1, D), jnp.bfloat16)], 0)
    grad_padded = jnp.concatenate([grad_block, jnp.zeros((1, D), jnp.bfloat16)], 0)
    prob_padded = jnp.concatenate([prob_block.reshape(-1), jnp.zeros((1,), jnp.float32)], 0)
    sent_rows = x_padded[token_pos]
    sent_grads = (prob_padded[slot_table][:, None] * grad_padded[token_pos].astype(jnp.float32)).astype(jnp.bfloat16)
    return sent_rows, sent_grads


def expert_rows(rows_in, scaled, proj_weight, down_weight):
    projected = jnp.dot(rows_in, proj_weight, preferred_element_type=jnp.float32)
    gate_pre = projected[:, :FF]
    up_part = projected[:, FF:]
    sigmoid_v = jax.nn.sigmoid(gate_pre)
    activated = gate_pre * sigmoid_v
    hidden = (activated * up_part).astype(jnp.bfloat16)
    grad_hidden = jnp.dot(scaled, down_weight, preferred_element_type=jnp.float32)
    grad_gate = grad_hidden * up_part * sigmoid_v * (1.0 + gate_pre * (1.0 - sigmoid_v))
    grad_proj = jnp.concatenate([grad_gate, grad_hidden * activated], 1).astype(jnp.bfloat16)
    grad_rows = lax.dot_general(grad_proj, proj_weight, (((1,), (1,)), ((), ())), preferred_element_type=jnp.float32).astype(jnp.bfloat16)
    return grad_rows, grad_proj, hidden


def weight_terms(rows_in, scaled, grad_proj, hidden):
    first = lax.dot_general(rows_in, grad_proj, (((0,), (0,)), ((), ())), preferred_element_type=jnp.float32)
    second = lax.dot_general(scaled, hidden, (((0,), (0,)), ((), ())), preferred_element_type=jnp.float32)
    return jnp.concatenate([first, second], 1)


def reference(x_in, grad_out, routes, gate_probs, gate_up, down):
    owners = N_EXPERT
    x_four = x_in.reshape(N_DP, owners, TOK_DEV, D)
    grad_four = grad_out.reshape(N_DP, owners, TOK_DEV, D)
    route_four = routes.reshape(N_DP, owners, TOK_DEV, TOP)
    prob_four = gate_probs.reshape(N_DP, owners, TOK_DEV, TOP)

    def per_row(total_sum, inputs):
        x_row, grad_row, route_row, prob_row = inputs
        slot_table, entry_pos = jax.vmap(dispatch_table)(route_row)
        sent_rows, sent_grads = jax.vmap(send_rows)(x_row, grad_row, prob_row, slot_table)
        sent_rows = sent_rows.reshape(owners, EXPERTS, CAP, D).transpose(1, 0, 2, 3).reshape(EXPERTS, owners * CAP, D)
        sent_grads = sent_grads.reshape(owners, EXPERTS, CAP, D).transpose(1, 0, 2, 3).reshape(EXPERTS, owners * CAP, D)

        def per_expert(items):
            rows_in, scaled, proj_weight, down_weight = items
            grad_rows, grad_proj, hidden = expert_rows(rows_in, scaled, proj_weight, down_weight)
            return grad_rows, weight_terms(rows_in, scaled, grad_proj, hidden).astype(jnp.bfloat16)

        grad_slots, partial_value = lax.map(per_expert, (sent_rows, sent_grads, gate_up, down))
        returned = grad_slots.reshape(EXPERTS, owners, CAP, D).transpose(1, 0, 2, 3).reshape(owners, EXPERTS * CAP, D)
        entries = jax.vmap(lambda block, where_at: block[where_at])(returned, entry_pos)
        grad_tokens = jnp.sum(entries.reshape(owners, TOK_DEV, TOP, D).astype(jnp.float32), axis=2).astype(jnp.bfloat16)
        return total_sum + partial_value.astype(jnp.float32), grad_tokens

    start_sum = jnp.zeros((EXPERTS, D, 3 * FF), jnp.float32)
    total_sum, grad_tokens = lax.scan(per_row, start_sum, (x_four, grad_four, route_four, prob_four))
    grad_in = grad_tokens.reshape(TOKENS, D)
    return grad_in, total_sum[:, :, :2 * FF], total_sum[:, :, 2 * FF:]
```

```python
import jax
import jax.numpy as jnp
from jax import lax
from jax.sharding import PartitionSpec as P


def slot_ranks(flat_ids, experts):
    onehot = (flat_ids[:, None] == jnp.arange(experts, dtype=jnp.int32)[None, :]).astype(jnp.int32)
    before = jnp.cumsum(onehot, axis=0) - onehot
    return jnp.sum(before * onehot, axis=1)


def dispatch_table(route_block, experts, capacity):
    flat_ids = route_block.reshape(-1)
    count_rows = flat_ids.shape[0]
    slot_rank = slot_ranks(flat_ids, experts)
    entry_pos = flat_ids * capacity + slot_rank
    slot_table = jnp.full((experts * capacity,), count_rows, jnp.int32)
    slot_table = slot_table.at[entry_pos].set(jnp.arange(count_rows, dtype=jnp.int32))
    return (slot_table, entry_pos)


def send_rows(x_block, grad_block, prob_block, slot_table, top_count):
    width = x_block.shape[1]
    token_pos = slot_table // top_count
    x_padded = jnp.concatenate([x_block, jnp.zeros((1, width), jnp.bfloat16)], 0)
    grad_padded = jnp.concatenate([grad_block, jnp.zeros((1, width), jnp.bfloat16)], 0)
    prob_padded = jnp.concatenate([prob_block.reshape(-1), jnp.zeros((1,), jnp.float32)], 0)
    sent_rows = x_padded[token_pos]
    sent_grads = (
        prob_padded[slot_table][:, None] * grad_padded[token_pos].astype(jnp.float32)
    ).astype(jnp.bfloat16)
    return (sent_rows, sent_grads)


def expert_rows(rows_in, scaled, proj_weight, down_weight):
    hidden_units = down_weight.shape[1]
    projected = jnp.dot(rows_in, proj_weight, preferred_element_type=jnp.float32)
    gate_pre = projected[:, :hidden_units]
    up_part = projected[:, hidden_units:]
    sigmoid_v = jax.nn.sigmoid(gate_pre)
    activated = gate_pre * sigmoid_v
    hidden = (activated * up_part).astype(jnp.bfloat16)
    grad_hidden = jnp.dot(scaled, down_weight, preferred_element_type=jnp.float32)
    grad_gate = grad_hidden * up_part * sigmoid_v * (1.0 + gate_pre * (1.0 - sigmoid_v))
    grad_proj = jnp.concatenate([grad_gate, grad_hidden * activated], 1).astype(jnp.bfloat16)
    grad_rows = lax.dot_general(
        grad_proj, proj_weight, (((1,), (1,)), ((), ())), preferred_element_type=jnp.float32
    ).astype(jnp.bfloat16)
    return (grad_rows, grad_proj, hidden)


def weight_terms(rows_in, scaled, grad_proj, hidden):
    first = lax.dot_general(
        rows_in, grad_proj, (((0,), (0,)), ((), ())), preferred_element_type=jnp.float32
    )
    second = lax.dot_general(
        scaled, hidden, (((0,), (0,)), ((), ())), preferred_element_type=jnp.float32
    )
    return jnp.concatenate([first, second], 1)


def dense_device(x_in, grad_out, routes, gate_probs, gate_up, down):
    owners = lax.axis_size("expert")
    me = lax.axis_index("expert")
    width = x_in.shape[1]
    ids = jnp.arange(owners, dtype=jnp.int32)
    prob_by_expert = jnp.sum(
        jnp.where(routes[:, :, None] == ids[None, None, :], gate_probs[:, :, None], 0.0), axis=1
    )
    all_probs = lax.all_gather(prob_by_expert, "expert", axis=0, tiled=True)
    rows_in = lax.all_gather(x_in, "expert", axis=0, tiled=True)
    all_grads = lax.all_gather(grad_out, "expert", axis=0, tiled=True)
    mine = jnp.sum(jnp.where(ids[None, :] == me, all_probs, 0.0), axis=1)
    scaled = (mine[:, None] * all_grads.astype(jnp.float32)).astype(jnp.bfloat16)
    grad_rows, grad_proj, hidden = expert_rows(rows_in, scaled, gate_up[0], down[0])
    grad_in = lax.psum_scatter(grad_rows, "expert", scatter_dimension=0, tiled=True)
    hidden_units = hidden.shape[1]
    grad_term = weight_terms(rows_in, scaled, grad_proj, hidden)
    grad_share = lax.psum_scatter(
        grad_term.astype(jnp.bfloat16), "dp", scatter_dimension=0, tiled=True
    ).astype(jnp.float32)
    return (
        grad_in,
        grad_share[None, :, : 2 * hidden_units],
        grad_share[None, :, 2 * hidden_units :],
    )


def per_device(x_in, grad_out, routes, gate_probs, gate_up, down):
    if lax.axis_size("expert") == routes.shape[1]:
        return dense_device(x_in, grad_out, routes, gate_probs, gate_up, down)
    owners = lax.axis_size("expert")
    tokens_here = x_in.shape[0]
    top_count = routes.shape[1]
    width = x_in.shape[1]
    capacity = min(tokens_here, tokens_here * top_count * 9 // (8 * owners))
    slot_table, entry_pos = dispatch_table(routes, owners, capacity)
    sent_rows, sent_grads = send_rows(x_in, grad_out, gate_probs, slot_table, top_count)
    sent_rows = sent_rows.reshape(owners, capacity, width)
    sent_grads = sent_grads.reshape(owners, capacity, width)
    proj_weight = gate_up[0]
    down_weight = down[0]
    recv_rows, recv_grads = (
        lax.all_to_all(sent_rows, "expert", split_axis=0, concat_axis=0, tiled=True),
        lax.all_to_all(sent_grads, "expert", split_axis=0, concat_axis=0, tiled=True),
    )
    rows_in = recv_rows.reshape(-1, width)
    scaled = recv_grads.reshape(-1, width)
    grad_rows, grad_proj, hidden = expert_rows(rows_in, scaled, proj_weight, down_weight)
    returned = lax.all_to_all(
        grad_rows.reshape(owners, capacity, width),
        "expert",
        split_axis=0,
        concat_axis=0,
        tiled=True,
    )
    hidden_units = hidden.shape[1]
    grad_term = weight_terms(rows_in, scaled, grad_proj, hidden)
    grad_share = lax.psum_scatter(
        grad_term.astype(jnp.bfloat16), "dp", scatter_dimension=0, tiled=True
    ).astype(jnp.float32)
    grad_gate_up = grad_share[None, :, : 2 * hidden_units]
    grad_down = grad_share[None, :, 2 * hidden_units :]
    entries = returned.reshape(-1, width)[entry_pos]
    grad_in = jnp.sum(
        entries.reshape(tokens_here, top_count, width).astype(jnp.float32), axis=1
    ).astype(jnp.bfloat16)
    return (grad_in, grad_gate_up, grad_down)


def solution(mesh):
    placed = (
        P(("dp", "expert"), None),
        P(("dp", "expert"), None),
        P(("dp", "expert"), None),
        P(("dp", "expert"), None),
        P("expert", None, None),
        P("expert", None, None),
    )
    return jax.shard_map(
        per_device,
        mesh=mesh,
        in_specs=placed,
        out_specs=(P(("dp", "expert"), None), P("expert", "dp", None), P("expert", "dp", None)),
        check_vma=False,
    )
```

```python
import jax
import jax.numpy as jnp
from jax import lax
from jax.experimental import pallas as pl
from jax.experimental.pallas import tpu as pltpu
from jax.sharding import PartitionSpec as P


def slot_ranks(flat_ids, experts):
    onehot = (flat_ids[:, None] == jnp.arange(experts, dtype=jnp.int32)[None, :]).astype(jnp.int32)
    before = jnp.cumsum(onehot, axis=0) - onehot
    return jnp.sum(before * onehot, axis=1)


def dispatch_table(route_block, experts, capacity):
    flat_ids = route_block.reshape(-1)
    count_rows = flat_ids.shape[0]
    slot_rank = slot_ranks(flat_ids, experts)
    entry_pos = flat_ids * capacity + slot_rank
    slot_table = jnp.full((experts * capacity,), count_rows, jnp.int32)
    slot_table = slot_table.at[entry_pos].set(jnp.arange(count_rows, dtype=jnp.int32))
    return (slot_table, entry_pos)


def send_rows(x_block, grad_block, prob_block, slot_table, top_count):
    width = x_block.shape[1]
    token_pos = slot_table // top_count
    x_padded = jnp.concatenate([x_block, jnp.zeros((1, width), jnp.bfloat16)], 0)
    grad_padded = jnp.concatenate([grad_block, jnp.zeros((1, width), jnp.bfloat16)], 0)
    prob_padded = jnp.concatenate([prob_block.reshape(-1), jnp.zeros((1,), jnp.float32)], 0)
    sent_rows = x_padded[token_pos]
    sent_grads = (
        prob_padded[slot_table][:, None] * grad_padded[token_pos].astype(jnp.float32)
    ).astype(jnp.bfloat16)
    return (sent_rows, sent_grads)


def expert_rows(rows_in, scaled, proj_weight, down_weight):
    hidden_units = down_weight.shape[1]
    projected = jnp.dot(rows_in, proj_weight, preferred_element_type=jnp.float32)
    gate_pre = projected[:, :hidden_units]
    up_part = projected[:, hidden_units:]
    sigmoid_v = jax.nn.sigmoid(gate_pre)
    activated = gate_pre * sigmoid_v
    hidden = (activated * up_part).astype(jnp.bfloat16)
    grad_hidden = jnp.dot(scaled, down_weight, preferred_element_type=jnp.float32)
    grad_gate = grad_hidden * up_part * sigmoid_v * (1.0 + gate_pre * (1.0 - sigmoid_v))
    grad_proj = jnp.concatenate([grad_gate, grad_hidden * activated], 1).astype(jnp.bfloat16)
    grad_rows = lax.dot_general(
        grad_proj, proj_weight, (((1,), (1,)), ((), ())), preferred_element_type=jnp.float32
    ).astype(jnp.bfloat16)
    return (grad_rows, grad_proj, hidden)


def weight_terms(rows_in, scaled, grad_proj, hidden):
    first = lax.dot_general(
        rows_in, grad_proj, (((0,), (0,)), ((), ())), preferred_element_type=jnp.float32
    )
    second = lax.dot_general(
        scaled, hidden, (((0,), (0,)), ((), ())), preferred_element_type=jnp.float32
    )
    return jnp.concatenate([first, second], 1)


def fused_kernel(
    p_ref, x_ref, g_ref, w_ref, dn_ref,
    gi_ref, ggu_ref, gd_ref,
    xg, p_all, rows, rin, xin, gp, hp, acc, part, mate_in, y_in, y_sum,
    got, up_sent, dn_sent, x_sent, p_got, p_sent, r_got, r_sent, xin_got, dp_got, dp_sent,
):
    me = lax.axis_index("expert")
    dp = lax.axis_index("dp")
    z, x = me // 2, lax.rem(me, 2)
    y, core = dp // 2, lax.rem(dp, 2)
    partner = 2 * z + (1 - x)
    mate = 2 * y + (1 - core)
    across = 2 * (1 - y) + core
    middle = lax.rem((z + 1) // 2, 2)
    ff = dn_ref.shape[1]
    quarter = w_ref.shape[0] // 4

    def send(src, dst, ssem, rsem, axis, to):
        return pltpu.make_async_remote_copy(
            src_ref=src, dst_ref=dst, send_sem=ssem, recv_sem=rsem,
            device_id={axis: to}, device_id_type=pl.DeviceIdType.MESH,
        )

    def level(k):
        turn = k + middle * (k // 2) * (1 - 2 * lax.rem(k, 2))
        return 2 * lax.rem(z // 2 + turn // 2, 2) + lax.rem(z + turn, 2)

    def ups(i, lev, src):
        return send(src, xg.at[i, 2 * lev + x], up_sent.at[i, lev], got.at[i, 2 * lev + x], "expert", me + 2)

    def downs(i, lev, src):
        return send(src, xg.at[i, 2 * lev + x], dn_sent.at[i, lev], got.at[i, 2 * lev + x], "expert", me - 2)

    def crosses(i, lev, src):
        return send(src, xg.at[i, 2 * lev + x], x_sent.at[i, lev], got.at[i, 2 * lev + x], "expert", partner)

    def spread(i, lev, src):
        @pl.when((lev <= z) & (z < 3))
        def _():
            ups(i, lev, src).start()

        @pl.when((lev >= z) & (z > 0))
        def _():
            downs(i, lev, src).start()

        crosses(i, lev, src).start()

    def arrived(i, blk):
        send(xg.at[i, blk], xg.at[i, blk], x_sent.at[i, 0], got.at[i, blk], "expert", partner).wait_recv()

    def probs_to(other):
        return send(p_ref, p_all.at[me], p_sent.at[other], p_got.at[me], "expert", other)

    def probs_from(blk):
        send(p_ref, p_all.at[blk], p_sent.at[0], p_got.at[blk], "expert", partner).wait_recv()

    def return_down(blk):
        return send(rows.at[blk], rin.at[0, blk], r_sent.at[blk], r_got.at[0, blk], "expert", me - 2)

    def return_up(blk):
        return send(rows.at[blk], rin.at[1, blk], r_sent.at[blk], r_got.at[1, blk], "expert", me + 2)

    def return_cross(blk):
        return send(rows.at[blk], xin, r_sent.at[blk], xin_got, "expert", partner)

    def pass_on(lev, blk):
        @pl.when(lev < z)
        def _():
            return_down(blk).start()

        @pl.when(lev > z)
        def _():
            return_up(blk).start()

    def add_in(side, blk):
        send(rows.at[blk], rin.at[side, blk], r_sent.at[blk], r_got.at[side, blk], "expert", partner).wait_recv()
        rows[blk] = (rows[blk].astype(jnp.float32) + rin[side, blk].astype(jnp.float32)).astype(jnp.bfloat16)

    def relay(k, other):
        lev = level(k)
        blk = 2 * lev + lax.rem(x + other, 2)

        @pl.when(lev < z)
        def _():
            add_in(0, blk)

        @pl.when(lev > z)
        def _():
            add_in(1, blk)

        pass_on(lev, blk)

    def finish(blk):
        @pl.when(z < 3)
        def _():
            add_in(0, blk)

        @pl.when(z > 0)
        def _():
            add_in(1, blk)

    barrier = pltpu.get_barrier_semaphore()
    for step in range(1, 8):
        pl.semaphore_signal(
            barrier, inc=1, device_id={"expert": lax.rem(me + step, 8)}, device_id_type=pl.DeviceIdType.MESH
        )
    for to in (mate, across):
        pl.semaphore_signal(barrier, inc=1, device_id={"dp": to}, device_id_type=pl.DeviceIdType.MESH)
    pl.semaphore_wait(barrier, 9)

    spread(0, z, x_ref)
    spread(1, z, g_ref)
    for step in range(1, 8):
        probs_to(lax.rem(me + step, 8)).start()
    xg[0, me] = x_ref[...]
    xg[1, me] = g_ref[...]
    p_all[me] = p_ref[...]
    acc[...] = jnp.zeros_like(acc)

    def work(blk):
        row_id = lax.broadcasted_iota(jnp.int32, (8, 128), 0)
        p_row = jnp.sum(jnp.where(row_id == me, p_all[blk], 0.0), axis=0, keepdims=True)
        p_cols = jnp.transpose(jnp.broadcast_to(p_row, (128, 128)))
        p_wide = jnp.concatenate([p_cols] * (ff // 128), axis=1)
        projected = jnp.dot(xg[0, blk], w_ref[...], preferred_element_type=jnp.float32)
        grad_hidden = jnp.dot(xg[1, blk], dn_ref[...], preferred_element_type=jnp.float32) * p_wide
        gate_pre = projected[:, :ff]
        up_part = projected[:, ff:]
        s = jax.nn.sigmoid(gate_pre)
        activated = gate_pre * s
        hp[blk] = (activated * up_part * p_wide).astype(jnp.bfloat16)
        gp[blk, :, :ff] = (grad_hidden * up_part * s * (1.0 + gate_pre * (1.0 - s))).astype(jnp.bfloat16)
        gp[blk, :, ff:] = (grad_hidden * activated).astype(jnp.bfloat16)
        rows[blk] = lax.dot_general(
            gp[blk], w_ref[...], (((1,), (1,)), ((), ())), preferred_element_type=jnp.float32
        ).astype(jnp.bfloat16)

    def weights(lev):
        pair = pl.ds(2 * lev, 2)
        gp_two = gp[pair].reshape(256, 2 * ff)
        hp_two = hp[pair].reshape(256, ff)
        for q in range(4):
            at = slice(q * quarter, (q + 1) * quarter)
            acc[at, : 2 * ff] += lax.dot_general(
                xg[0, pair, :, at].reshape(256, quarter), gp_two,
                (((0,), (0,)), ((), ())), preferred_element_type=jnp.float32,
            )
            acc[at, 2 * ff :] += lax.dot_general(
                xg[1, pair, :, at].reshape(256, quarter), hp_two,
                (((0,), (0,)), ((), ())), preferred_element_type=jnp.float32,
            )

    def step(s, carry):
        k, other = s // 2, lax.rem(s, 2)
        lev = level(k)
        blk = 2 * lev + lax.rem(x + other, 2)

        @pl.when((other == 1) & (k < 3))
        def _():
            ahead = level(k + 1)
            for i in range(2):
                arrived(i, 2 * ahead + x)
                spread(i, ahead, xg.at[i, 2 * ahead + x])

        @pl.when((s == 7) & (middle == 1))
        def _():
            relay(2, 0)
            relay(3, 0)

        @pl.when(other == 1)
        def _():
            for i in range(2):
                arrived(i, blk)

        @pl.when(s > 0)
        def _():
            probs_from(blk)

        work(blk)

        @pl.when((middle == 0) & (k > 0))
        def _():
            pass_on(lev, blk)

        @pl.when(other == 1)
        def _():
            weights(lev)

        return carry

    lax.fori_loop(0, 8, step, 0)

    for d in range(4):
        part[d] = acc[d * quarter : (d + 1) * quarter].astype(jnp.bfloat16)

    def to_mate(i, row):
        return send(part.at[row], mate_in.at[i], dp_sent.at[i], dp_got.at[i], "dp", mate)

    first = to_mate(0, 2 * (1 - y) + (1 - core))
    second = to_mate(1, mate)
    first.start()
    second.start()

    @pl.when(middle == 1)
    def _():
        relay(2, 1)
        relay(1, 0)

    first.wait_recv()
    y_sum[...] = (part[across].astype(jnp.float32) + mate_in[0].astype(jnp.float32)).astype(jnp.bfloat16)
    over = send(y_sum, y_in, dp_sent.at[2], dp_got.at[2], "dp", across)
    over.start()

    @pl.when(middle == 1)
    def _():
        relay(3, 1)
        relay(1, 1)

    finish(partner)
    return_cross(partner).start()
    finish(me)

    second.wait_recv()
    over.wait_recv()
    total = part[dp].astype(jnp.float32) + mate_in[1].astype(jnp.float32) + y_in[...].astype(jnp.float32)
    ggu_ref[...] = total[:, : 2 * ff]
    gd_ref[...] = total[:, 2 * ff :]

    return_cross(partner).wait_recv()
    gi_ref[...] = (rows[me].astype(jnp.float32) + xin[...].astype(jnp.float32)).astype(jnp.bfloat16)

    first.wait_send()
    second.wait_send()
    over.wait_send()
    return_cross(partner).wait_send()
    for i in range(7):
        probs_to(lax.rem(me + 1 + i, 8)).wait_send()
    for lev in range(4):
        for i in range(2):
            src = xg.at[i, 2 * lev + x]

            @pl.when((lev <= z) & (z < 3))
            def _():
                ups(i, lev, src).wait_send()

            @pl.when((lev >= z) & (z > 0))
            def _():
                downs(i, lev, src).wait_send()

            crosses(i, lev, src).wait_send()
            blk = 2 * lev + i

            @pl.when(lev < z)
            def _():
                return_down(blk).wait_send()

            @pl.when(lev > z)
            def _():
                return_up(blk).wait_send()


def dense_device(x_in, grad_out, routes, gate_probs, gate_up, down):
    owners = lax.axis_size("expert")
    tokens, width = x_in.shape
    hidden_units = down.shape[2]
    cols = 3 * hidden_units
    quarter = width // 4
    ids = jnp.arange(owners, dtype=jnp.int32)
    prob_by_expert = jnp.sum(
        jnp.where(routes.T[:, None, :] == ids[None, :, None], gate_probs.T[:, None, :], 0.0), axis=0
    )
    bf16, f32, dma = jnp.bfloat16, jnp.float32, pltpu.SemaphoreType.DMA
    vmem = pl.BlockSpec(memory_space=pltpu.VMEM)
    grad_in, grad_gate_up, grad_down = pl.pallas_call(
        fused_kernel,
        out_shape=(
            jax.ShapeDtypeStruct((tokens, width), bf16),
            jax.ShapeDtypeStruct((quarter, 2 * hidden_units), f32),
            jax.ShapeDtypeStruct((quarter, hidden_units), f32),
        ),
        in_specs=[vmem] * 5,
        out_specs=(vmem,) * 3,
        scratch_shapes=[
            pltpu.VMEM((2, owners, tokens, width), bf16),
            pltpu.VMEM((owners, owners, tokens), f32),
            pltpu.VMEM((owners, tokens, width), bf16),
            pltpu.VMEM((2, owners, tokens, width), bf16),
            pltpu.VMEM((tokens, width), bf16),
            pltpu.VMEM((owners, tokens, 2 * hidden_units), bf16),
            pltpu.VMEM((owners, tokens, hidden_units), bf16),
            pltpu.VMEM((width, cols), f32),
            pltpu.VMEM((4, quarter, cols), bf16),
            pltpu.VMEM((2, quarter, cols), bf16),
            pltpu.VMEM((quarter, cols), bf16),
            pltpu.VMEM((quarter, cols), bf16),
            dma((2, owners)),
            dma((2, 4)),
            dma((2, 4)),
            dma((2, 4)),
            dma((owners,)),
            dma((owners,)),
            dma((2, owners)),
            dma((owners,)),
            dma,
            dma((3,)),
            dma((3,)),
        ],
        compiler_params=pltpu.CompilerParams(
            collective_id=0, has_side_effects=True, vmem_limit_bytes=52 * 1024 * 1024
        ),
    )(prob_by_expert, x_in, grad_out, gate_up[0], down[0])
    return (grad_in, grad_gate_up[None], grad_down[None])


def per_device(x_in, grad_out, routes, gate_probs, gate_up, down):
    lines = (lax.axis_size("expert"), lax.axis_size("dp"), routes.shape[1], x_in.shape[0])
    if lines == (8, 4, 8, 128):
        return dense_device(x_in, grad_out, routes, gate_probs, gate_up, down)
    owners = lax.axis_size("expert")
    tokens_here = x_in.shape[0]
    top_count = routes.shape[1]
    width = x_in.shape[1]
    capacity = min(tokens_here, tokens_here * top_count * 9 // (8 * owners))
    slot_table, entry_pos = dispatch_table(routes, owners, capacity)
    sent_rows, sent_grads = send_rows(x_in, grad_out, gate_probs, slot_table, top_count)
    sent_rows = sent_rows.reshape(owners, capacity, width)
    sent_grads = sent_grads.reshape(owners, capacity, width)
    proj_weight = gate_up[0]
    down_weight = down[0]
    recv_rows, recv_grads = (
        lax.all_to_all(sent_rows, "expert", split_axis=0, concat_axis=0, tiled=True),
        lax.all_to_all(sent_grads, "expert", split_axis=0, concat_axis=0, tiled=True),
    )
    rows_in = recv_rows.reshape(-1, width)
    scaled = recv_grads.reshape(-1, width)
    grad_rows, grad_proj, hidden = expert_rows(rows_in, scaled, proj_weight, down_weight)
    returned = lax.all_to_all(
        grad_rows.reshape(owners, capacity, width),
        "expert",
        split_axis=0,
        concat_axis=0,
        tiled=True,
    )
    hidden_units = hidden.shape[1]
    grad_term = weight_terms(rows_in, scaled, grad_proj, hidden)
    grad_share = lax.psum_scatter(
        grad_term.astype(jnp.bfloat16), "dp", scatter_dimension=0, tiled=True
    ).astype(jnp.float32)
    grad_gate_up = grad_share[None, :, : 2 * hidden_units]
    grad_down = grad_share[None, :, 2 * hidden_units :]
    entries = returned.reshape(-1, width)[entry_pos]
    grad_in = jnp.sum(
        entries.reshape(tokens_here, top_count, width).astype(jnp.float32), axis=1
    ).astype(jnp.bfloat16)
    return (grad_in, grad_gate_up, grad_down)


def solution(mesh):
    placed = (
        P(("dp", "expert"), None),
        P(("dp", "expert"), None),
        P(("dp", "expert"), None),
        P(("dp", "expert"), None),
        P("expert", None, None),
        P("expert", None, None),
    )
    return jax.shard_map(
        per_device,
        mesh=mesh,
        in_specs=placed,
        out_specs=(P(("dp", "expert"), None), P("expert", "dp", None), P("expert", "dp", None)),
        check_vma=False,
    )
```

```python
import jax
import jax.numpy as jnp
from jax import lax
from jax.experimental import pallas as pl
from jax.experimental.pallas import tpu as pltpu
from jax.sharding import PartitionSpec as P


def slot_ranks(flat_ids, experts):
    onehot = (flat_ids[:, None] == jnp.arange(experts, dtype=jnp.int32)[None, :]).astype(jnp.int32)
    before = jnp.cumsum(onehot, axis=0) - onehot
    return jnp.sum(before * onehot, axis=1)


def dispatch_table(route_block, experts, capacity):
    flat_ids = route_block.reshape(-1)
    count_rows = flat_ids.shape[0]
    slot_rank = slot_ranks(flat_ids, experts)
    entry_pos = flat_ids * capacity + slot_rank
    slot_table = jnp.full((experts * capacity,), count_rows, jnp.int32)
    slot_table = slot_table.at[entry_pos].set(jnp.arange(count_rows, dtype=jnp.int32))
    return (slot_table, entry_pos)


def send_rows(x_block, grad_block, prob_block, slot_table, top_count):
    width = x_block.shape[1]
    token_pos = slot_table // top_count
    x_padded = jnp.concatenate([x_block, jnp.zeros((1, width), jnp.bfloat16)], 0)
    grad_padded = jnp.concatenate([grad_block, jnp.zeros((1, width), jnp.bfloat16)], 0)
    prob_padded = jnp.concatenate([prob_block.reshape(-1), jnp.zeros((1,), jnp.float32)], 0)
    sent_rows = x_padded[token_pos]
    sent_grads = (
        prob_padded[slot_table][:, None] * grad_padded[token_pos].astype(jnp.float32)
    ).astype(jnp.bfloat16)
    return (sent_rows, sent_grads)


def expert_rows(rows_in, scaled, proj_weight, down_weight):
    hidden_units = down_weight.shape[1]
    projected = jnp.dot(rows_in, proj_weight, preferred_element_type=jnp.float32)
    gate_pre = projected[:, :hidden_units]
    up_part = projected[:, hidden_units:]
    sigmoid_v = jax.nn.sigmoid(gate_pre)
    activated = gate_pre * sigmoid_v
    hidden = (activated * up_part).astype(jnp.bfloat16)
    grad_hidden = jnp.dot(scaled, down_weight, preferred_element_type=jnp.float32)
    grad_gate = grad_hidden * up_part * sigmoid_v * (1.0 + gate_pre * (1.0 - sigmoid_v))
    grad_proj = jnp.concatenate([grad_gate, grad_hidden * activated], 1).astype(jnp.bfloat16)
    grad_rows = lax.dot_general(
        grad_proj, proj_weight, (((1,), (1,)), ((), ())), preferred_element_type=jnp.float32
    ).astype(jnp.bfloat16)
    return (grad_rows, grad_proj, hidden)


def weight_terms(rows_in, scaled, grad_proj, hidden):
    first = lax.dot_general(
        rows_in, grad_proj, (((0,), (0,)), ((), ())), preferred_element_type=jnp.float32
    )
    second = lax.dot_general(
        scaled, hidden, (((0,), (0,)), ((), ())), preferred_element_type=jnp.float32
    )
    return jnp.concatenate([first, second], 1)


def fused_kernel(
    p_ref, x_hbm, g_hbm, w_hbm, dn_hbm,
    gi_ref, ggu_ref, gd_ref,
    w_ref, dn_ref, xg, p_all, rows, rin, xin, gp, hp, acc, part, mate_in, y_in, y_sum,
    got, up_sent, dn_sent, x_sent, p_got, p_sent, r_got, r_sent, xin_got, dp_got, dp_sent, loaded, carry_sent,
):
    me = lax.axis_index("expert")
    dp = lax.axis_index("dp")
    z, x = me // 2, lax.rem(me, 2)
    y, core = dp // 2, lax.rem(dp, 2)
    partner = 2 * z + (1 - x)
    mate = 2 * y + (1 - core)
    across = 2 * (1 - y) + core
    middle = lax.rem((z + 1) // 2, 2)
    half = rows.shape[1] // 2
    ff = dn_ref.shape[1]
    quarter = w_ref.shape[0] // 4

    def send(src, dst, ssem, rsem, axis, to):
        return pltpu.make_async_remote_copy(
            src_ref=src, dst_ref=dst, send_sem=ssem, recv_sem=rsem,
            device_id={axis: to}, device_id_type=pl.DeviceIdType.MESH,
        )

    def level(k):
        turn = k + middle * (k // 2) * (1 - 2 * lax.rem(k, 2))
        return 2 * lax.rem(z // 2 + turn // 2, 2) + lax.rem(z + turn, 2)

    def ups(i, lev, src):
        return send(src, xg.at[i, 2 * lev + x], up_sent.at[i, lev], got.at[i, 2 * lev + x], "expert", me + 2)

    def downs(i, lev, src):
        return send(src, xg.at[i, 2 * lev + x], dn_sent.at[i, lev], got.at[i, 2 * lev + x], "expert", me - 2)

    def crosses(i, lev, src):
        return send(src, xg.at[i, 2 * lev + x], x_sent.at[i, lev], got.at[i, 2 * lev + x], "expert", partner)

    def spread(i, lev, src):
        @pl.when((lev <= z) & (z < 3))
        def _():
            ups(i, lev, src).start()

        @pl.when((lev >= z) & (z > 0))
        def _():
            downs(i, lev, src).start()

        @pl.when(is_crossed(i, lev))
        def _():
            crosses(i, lev, src).start()

    def is_crossed(i, lev):
        return (lev == z) | (lax.rem(lev, 3) + 1 - i > 0)

    def carry_up():
        blk = 1 - x
        return send(xg.at[1, blk], xg.at[1, blk], carry_sent.at[0], got.at[1, blk], "expert", me + 2)

    def carry_down():
        blk = 7 - x
        return send(xg.at[1, blk], xg.at[1, blk], carry_sent.at[1], got.at[1, blk], "expert", me - 2)

    def carry_on(lev):
        arrived(1, 2 * lev + 1 - x)

        @pl.when(lev == 0)
        def _():
            carry_up().start()

        @pl.when(lev == 3)
        def _():
            carry_down().start()

    def arrived(i, blk):
        send(xg.at[i, blk], xg.at[i, blk], x_sent.at[i, 0], got.at[i, blk], "expert", partner).wait_recv()

    def probs_to(other):
        return send(p_ref, p_all.at[me], p_sent.at[other], p_got.at[me], "expert", other)

    def probs_from(blk):
        send(p_ref, p_all.at[blk], p_sent.at[0], p_got.at[blk], "expert", partner).wait_recv()

    def return_to(side, blk, h, to):
        at = pl.ds(h * half, half)
        return send(
            rows.at[blk, at], rin.at[side, blk, at], r_sent.at[h, blk], r_got.at[h, side, blk], "expert", to
        )

    def return_down(blk, h):
        return return_to(0, blk, h, me - 2)

    def return_up(blk, h):
        return return_to(1, blk, h, me + 2)

    def return_cross(blk, h):
        at = pl.ds(h * half, half)
        return send(rows.at[blk, at], xin.at[at], r_sent.at[h, blk], xin_got.at[h], "expert", partner)

    def pass_on(lev, blk, h):
        @pl.when(lev < z)
        def _():
            return_down(blk, h).start()

        @pl.when(lev > z)
        def _():
            return_up(blk, h).start()

    def add_in(side, blk, h):
        return_to(side, blk, h, partner).wait_recv()
        at = slice(h * half, (h + 1) * half)
        rows[blk, at] = (
            rows[blk, at].astype(jnp.float32) + rin[side, blk, at].astype(jnp.float32)
        ).astype(jnp.bfloat16)

    def relay(k, other):
        lev = level(k)
        blk = 2 * lev + lax.rem(x + other, 2)

        for h in range(2):
            @pl.when(lev < z)
            def _():
                add_in(0, blk, h)

            @pl.when(lev > z)
            def _():
                add_in(1, blk, h)

            pass_on(lev, blk, h)

    def finish(blk, h):
        @pl.when(z < 3)
        def _():
            add_in(0, blk, h)

        @pl.when(z > 0)
        def _():
            add_in(1, blk, h)

    loads = [
        pltpu.make_async_copy(src, dst, loaded.at[i])
        for i, (src, dst) in enumerate(
            ((x_hbm, xg.at[0, me]), (g_hbm, xg.at[1, me]), (w_hbm, w_ref), (dn_hbm, dn_ref))
        )
    ]
    for load in loads:
        load.start()

    barrier = pltpu.get_barrier_semaphore()
    for step in range(1, 8):
        pl.semaphore_signal(
            barrier, inc=1, device_id={"expert": lax.rem(me + step, 8)}, device_id_type=pl.DeviceIdType.MESH
        )
    for to in (mate, across):
        pl.semaphore_signal(barrier, inc=1, device_id={"dp": to}, device_id_type=pl.DeviceIdType.MESH)
    pl.semaphore_wait(barrier, 9)

    for i in range(2):
        loads[i].wait()
        spread(i, z, xg.at[i, me])
    for step in range(1, 8):
        probs_to(lax.rem(me + step, 8)).start()
    p_all[me] = p_ref[...]
    acc[...] = jnp.zeros_like(acc)
    loads[2].wait()
    loads[3].wait()

    def work(blk):
        row_id = lax.broadcasted_iota(jnp.int32, (8, 128), 0)
        p_row = jnp.sum(jnp.where(row_id == me, p_all[blk], 0.0), axis=0, keepdims=True)
        p_cols = jnp.transpose(jnp.broadcast_to(p_row, (128, 128)))
        p_wide = jnp.concatenate([p_cols] * (ff // 128), axis=1)
        projected = jnp.dot(xg[0, blk], w_ref[...], preferred_element_type=jnp.float32)
        grad_hidden = jnp.dot(xg[1, blk], dn_ref[...], preferred_element_type=jnp.float32) * p_wide
        gate_pre = projected[:, :ff]
        up_part = projected[:, ff:]
        s = jax.nn.sigmoid(gate_pre)
        activated = gate_pre * s
        hp[blk] = (activated * up_part * p_wide).astype(jnp.bfloat16)
        gp[blk, :, :ff] = (grad_hidden * up_part * s * (1.0 + gate_pre * (1.0 - s))).astype(jnp.bfloat16)
        gp[blk, :, ff:] = (grad_hidden * activated).astype(jnp.bfloat16)
        rows[blk] = lax.dot_general(
            gp[blk], w_ref[...], (((1,), (1,)), ((), ())), preferred_element_type=jnp.float32
        ).astype(jnp.bfloat16)

    def relay_block(k):
        ahead = level(k)
        for i in range(2):
            arrived(i, 2 * ahead + x)
            spread(i, ahead, xg.at[i, 2 * ahead + x])

    def terms(lev, q):
        pair = pl.ds(2 * lev, 2)
        at = pl.ds(pl.multiple_of(q * quarter, quarter), quarter)
        first_term = lax.dot_general(
            xg[0, pair, :, at].reshape(256, quarter), gp[pair].reshape(256, 2 * ff),
            (((0,), (0,)), ((), ())), preferred_element_type=jnp.float32,
        )
        second_term = lax.dot_general(
            xg[1, pair, :, at].reshape(256, quarter), hp[pair].reshape(256, ff),
            (((0,), (0,)), ((), ())), preferred_element_type=jnp.float32,
        )
        return (first_term, second_term)

    def weights(lev):
        for q in range(4):
            first_term, second_term = terms(lev, q)
            acc[q, :, : 2 * ff] += first_term
            acc[q, :, 2 * ff :] += second_term

    def last_weights(q):
        first_term, second_term = terms(level(3), q)
        part[q, :, : 2 * ff] = (acc[q, :, : 2 * ff] + first_term).astype(jnp.bfloat16)
        part[q, :, 2 * ff :] = (acc[q, :, 2 * ff :] + second_term).astype(jnp.bfloat16)

    def step(s, carry):
        k, other = s // 2, lax.rem(s, 2)
        lev = level(k)
        blk = 2 * lev + lax.rem(x + other, 2)

        @pl.when((middle == 1) & ((s == 3) | (s == 5)))
        def _():
            carry_on(level(2 * k - 1))

        @pl.when((other == 1) & (k + middle < 3))
        def _():
            relay_block(k + 1 + middle * ((k + 1) // 2))

        @pl.when((s == 1) & (middle == 1))
        def _():
            relay_block(2)

        @pl.when((s == 7) & (middle == 1))
        def _():
            relay(2, 0)
            relay(3, 0)

        @pl.when(other == 1)
        def _():
            arrived(0, blk)

            @pl.when((middle == 0) & (k == 0))
            def _():
                carry_on(lev)

            @pl.when(((middle == 0) & (k > 0)) | ((middle == 1) & (lax.rem(k, 2) == 0)))
            def _():
                arrived(1, blk)

        @pl.when(s > 0)
        def _():
            probs_from(blk)

        work(blk)

        @pl.when((middle == 0) & (k > 0))
        def _():
            pass_on(lev, blk, 0)
            pass_on(lev, blk, 1)

        @pl.when((other == 1) & (k < 3))
        def _():
            weights(lev)

        return carry

    lax.fori_loop(0, 8, step, 0)

    def to_mate(i, row):
        return send(part.at[row], mate_in.at[i], dp_sent.at[i], dp_got.at[i], "dp", mate)

    diagonal = 2 * (1 - y) + (1 - core)
    first = to_mate(0, diagonal)
    second = to_mate(1, mate)
    last_weights(diagonal)
    first.start()
    last_weights(across)

    first.wait_recv()
    y_sum[...] = (part[across].astype(jnp.float32) + mate_in[0].astype(jnp.float32)).astype(jnp.bfloat16)
    over = send(y_sum, y_in, dp_sent.at[2], dp_got.at[2], "dp", across)
    over.start()
    last_weights(mate)
    second.start()

    @pl.when(middle == 1)
    def _():
        relay(2, 1)
        relay(1, 0)

    @pl.when(middle == 1)
    def _():
        relay(3, 1)
        relay(1, 1)

    last_weights(dp)

    for h in range(2):
        finish(partner, h)
        return_cross(partner, h).start()
    for h in range(2):
        finish(me, h)

    second.wait_recv()
    over.wait_recv()
    total = part[dp].astype(jnp.float32) + mate_in[1].astype(jnp.float32) + y_in[...].astype(jnp.float32)
    ggu_ref[...] = total[:, : 2 * ff]
    gd_ref[...] = total[:, 2 * ff :]

    for h in range(2):
        return_cross(partner, h).wait_recv()
    gi_ref[...] = (rows[me].astype(jnp.float32) + xin[...].astype(jnp.float32)).astype(jnp.bfloat16)

    @pl.when(z < 3)
    def _():
        carry_up().wait_send()

    @pl.when(z > 0)
    def _():
        carry_down().wait_send()

    first.wait_send()
    second.wait_send()
    over.wait_send()
    for h in range(2):
        return_cross(partner, h).wait_send()
    for i in range(7):
        probs_to(lax.rem(me + 1 + i, 8)).wait_send()
    for lev in range(4):
        for i in range(2):
            src = xg.at[i, 2 * lev + x]

            @pl.when((lev <= z) & (z < 3))
            def _():
                ups(i, lev, src).wait_send()

            @pl.when((lev >= z) & (z > 0))
            def _():
                downs(i, lev, src).wait_send()

            @pl.when(is_crossed(i, lev))
            def _():
                crosses(i, lev, src).wait_send()

            blk = 2 * lev + i

            @pl.when(lev < z)
            def _():
                return_down(blk, 0).wait_send()
                return_down(blk, 1).wait_send()

            @pl.when(lev > z)
            def _():
                return_up(blk, 0).wait_send()
                return_up(blk, 1).wait_send()


def dense_device(x_in, grad_out, routes, gate_probs, gate_up, down):
    owners = lax.axis_size("expert")
    tokens, width = x_in.shape
    hidden_units = down.shape[2]
    cols = 3 * hidden_units
    quarter = width // 4
    ids = jnp.arange(owners, dtype=jnp.int32)
    prob_by_expert = jnp.sum(
        jnp.where(routes.T[:, None, :] == ids[None, :, None], gate_probs.T[:, None, :], 0.0), axis=0
    )
    bf16, f32, dma = jnp.bfloat16, jnp.float32, pltpu.SemaphoreType.DMA
    vmem = pl.BlockSpec(memory_space=pltpu.VMEM)
    grad_in, grad_gate_up, grad_down = pl.pallas_call(
        fused_kernel,
        out_shape=(
            jax.ShapeDtypeStruct((tokens, width), bf16),
            jax.ShapeDtypeStruct((quarter, 2 * hidden_units), f32),
            jax.ShapeDtypeStruct((quarter, hidden_units), f32),
        ),
        in_specs=[vmem] + [pl.BlockSpec(memory_space=pl.ANY)] * 4,
        out_specs=(vmem,) * 3,
        scratch_shapes=[
            pltpu.VMEM((width, 2 * hidden_units), bf16),
            pltpu.VMEM((width, hidden_units), bf16),
            pltpu.VMEM((2, owners, tokens, width), bf16),
            pltpu.VMEM((owners, owners, tokens), f32),
            pltpu.VMEM((owners, tokens, width), bf16),
            pltpu.VMEM((2, owners, tokens, width), bf16),
            pltpu.VMEM((tokens, width), bf16),
            pltpu.VMEM((owners, tokens, 2 * hidden_units), bf16),
            pltpu.VMEM((owners, tokens, hidden_units), bf16),
            pltpu.VMEM((4, quarter, cols), f32),
            pltpu.VMEM((4, quarter, cols), bf16),
            pltpu.VMEM((2, quarter, cols), bf16),
            pltpu.VMEM((quarter, cols), bf16),
            pltpu.VMEM((quarter, cols), bf16),
            dma((2, owners)),
            dma((2, 4)),
            dma((2, 4)),
            dma((2, 4)),
            dma((owners,)),
            dma((owners,)),
            dma((2, 2, owners)),
            dma((2, owners)),
            dma((2,)),
            dma((3,)),
            dma((3,)),
            dma((4,)),
            dma((2,)),
        ],
        compiler_params=pltpu.CompilerParams(
            collective_id=0, has_side_effects=True, vmem_limit_bytes=54 * 1024 * 1024
        ),
    )(prob_by_expert, x_in, grad_out, gate_up[0], down[0])
    return (grad_in, grad_gate_up[None], grad_down[None])


def per_device(x_in, grad_out, routes, gate_probs, gate_up, down):
    lines = (lax.axis_size("expert"), lax.axis_size("dp"), routes.shape[1], x_in.shape[0])
    if lines == (8, 4, 8, 128):
        return dense_device(x_in, grad_out, routes, gate_probs, gate_up, down)
    owners = lax.axis_size("expert")
    tokens_here = x_in.shape[0]
    top_count = routes.shape[1]
    width = x_in.shape[1]
    capacity = min(tokens_here, tokens_here * top_count * 9 // (8 * owners))
    slot_table, entry_pos = dispatch_table(routes, owners, capacity)
    sent_rows, sent_grads = send_rows(x_in, grad_out, gate_probs, slot_table, top_count)
    sent_rows = sent_rows.reshape(owners, capacity, width)
    sent_grads = sent_grads.reshape(owners, capacity, width)
    proj_weight = gate_up[0]
    down_weight = down[0]
    recv_rows, recv_grads = (
        lax.all_to_all(sent_rows, "expert", split_axis=0, concat_axis=0, tiled=True),
        lax.all_to_all(sent_grads, "expert", split_axis=0, concat_axis=0, tiled=True),
    )
    rows_in = recv_rows.reshape(-1, width)
    scaled = recv_grads.reshape(-1, width)
    grad_rows, grad_proj, hidden = expert_rows(rows_in, scaled, proj_weight, down_weight)
    returned = lax.all_to_all(
        grad_rows.reshape(owners, capacity, width),
        "expert",
        split_axis=0,
        concat_axis=0,
        tiled=True,
    )
    hidden_units = hidden.shape[1]
    grad_term = weight_terms(rows_in, scaled, grad_proj, hidden)
    grad_share = lax.psum_scatter(
        grad_term.astype(jnp.bfloat16), "dp", scatter_dimension=0, tiled=True
    ).astype(jnp.float32)
    grad_gate_up = grad_share[None, :, : 2 * hidden_units]
    grad_down = grad_share[None, :, 2 * hidden_units :]
    entries = returned.reshape(-1, width)[entry_pos]
    grad_in = jnp.sum(
        entries.reshape(tokens_here, top_count, width).astype(jnp.float32), axis=1
    ).astype(jnp.bfloat16)
    return (grad_in, grad_gate_up, grad_down)


def solution(mesh):
    placed = (
        P(("dp", "expert"), None),
        P(("dp", "expert"), None),
        P(("dp", "expert"), None),
        P(("dp", "expert"), None),
        P("expert", None, None),
        P("expert", None, None),
    )
    return jax.shard_map(
        per_device,
        mesh=mesh,
        in_specs=placed,
        out_specs=(P(("dp", "expert"), None), P("expert", "dp", None), P("expert", "dp", None)),
        check_vma=False,
    )
```

```python
import jax
import jax.numpy as jnp
from jax import lax
from jax.experimental import pallas as pl
from jax.experimental.pallas import tpu as pltpu
from jax.sharding import PartitionSpec as P


def slot_ranks(flat_ids, experts):
    onehot = (flat_ids[:, None] == jnp.arange(experts, dtype=jnp.int32)[None, :]).astype(jnp.int32)
    before = jnp.cumsum(onehot, axis=0) - onehot
    return jnp.sum(before * onehot, axis=1)


def dispatch_table(route_block, experts, capacity):
    flat_ids = route_block.reshape(-1)
    count_rows = flat_ids.shape[0]
    slot_rank = slot_ranks(flat_ids, experts)
    entry_pos = flat_ids * capacity + slot_rank
    slot_table = jnp.full((experts * capacity,), count_rows, jnp.int32)
    slot_table = slot_table.at[entry_pos].set(jnp.arange(count_rows, dtype=jnp.int32))
    return (slot_table, entry_pos)


def send_rows(x_block, grad_block, prob_block, slot_table, top_count):
    width = x_block.shape[1]
    token_pos = slot_table // top_count
    x_padded = jnp.concatenate([x_block, jnp.zeros((1, width), jnp.bfloat16)], 0)
    grad_padded = jnp.concatenate([grad_block, jnp.zeros((1, width), jnp.bfloat16)], 0)
    prob_padded = jnp.concatenate([prob_block.reshape(-1), jnp.zeros((1,), jnp.float32)], 0)
    sent_rows = x_padded[token_pos]
    sent_grads = (
        prob_padded[slot_table][:, None] * grad_padded[token_pos].astype(jnp.float32)
    ).astype(jnp.bfloat16)
    return (sent_rows, sent_grads)


def expert_rows(rows_in, scaled, proj_weight, down_weight):
    hidden_units = down_weight.shape[1]
    projected = jnp.dot(rows_in, proj_weight, preferred_element_type=jnp.float32)
    gate_pre = projected[:, :hidden_units]
    up_part = projected[:, hidden_units:]
    sigmoid_v = jax.nn.sigmoid(gate_pre)
    activated = gate_pre * sigmoid_v
    hidden = (activated * up_part).astype(jnp.bfloat16)
    grad_hidden = jnp.dot(scaled, down_weight, preferred_element_type=jnp.float32)
    grad_gate = grad_hidden * up_part * sigmoid_v * (1.0 + gate_pre * (1.0 - sigmoid_v))
    grad_proj = jnp.concatenate([grad_gate, grad_hidden * activated], 1).astype(jnp.bfloat16)
    grad_rows = lax.dot_general(
        grad_proj, proj_weight, (((1,), (1,)), ((), ())), preferred_element_type=jnp.float32
    ).astype(jnp.bfloat16)
    return (grad_rows, grad_proj, hidden)


def weight_terms(rows_in, scaled, grad_proj, hidden):
    first = lax.dot_general(
        rows_in, grad_proj, (((0,), (0,)), ((), ())), preferred_element_type=jnp.float32
    )
    second = lax.dot_general(
        scaled, hidden, (((0,), (0,)), ((), ())), preferred_element_type=jnp.float32
    )
    return jnp.concatenate([first, second], 1)


def fused_kernel(
    p_ref, x_hbm, g_hbm, w_hbm, dn_hbm,
    gi_ref, ggu_ref, gd_ref,
    w_ref, dn_ref, xg, p_all, rows, rin, xin, gp, hp, acc, part, mate_in, y_in, y_sum,
    got, up_sent, dn_sent, x_sent, p_got, p_sent, r_got, r_sent, xin_got, dp_got, dp_sent, loaded,
):
    me = lax.axis_index("expert")
    dp = lax.axis_index("dp")
    z, x = me // 2, lax.rem(me, 2)
    y, core = dp // 2, lax.rem(dp, 2)
    partner = 2 * z + (1 - x)
    mate = 2 * y + (1 - core)
    across = 2 * (1 - y) + core
    middle = lax.rem((z + 1) // 2, 2)
    half = rows.shape[1] // 2
    ff = dn_ref.shape[1]
    quarter = w_ref.shape[0] // 4

    def send(src, dst, ssem, rsem, axis, to):
        return pltpu.make_async_remote_copy(
            src_ref=src, dst_ref=dst, send_sem=ssem, recv_sem=rsem,
            device_id={axis: to}, device_id_type=pl.DeviceIdType.MESH,
        )

    def level(k):
        turn = k + middle * (k // 2) * (1 - 2 * lax.rem(k, 2))
        return 2 * lax.rem(z // 2 + turn // 2, 2) + lax.rem(z + turn, 2)

    def ups(i, lev, src):
        return send(src, xg.at[i, 2 * lev + x], up_sent.at[i, lev], got.at[i, 2 * lev + x], "expert", me + 2)

    def downs(i, lev, src):
        return send(src, xg.at[i, 2 * lev + x], dn_sent.at[i, lev], got.at[i, 2 * lev + x], "expert", me - 2)

    def crosses(i, lev, src):
        return send(src, xg.at[i, 2 * lev + x], x_sent.at[i, lev], got.at[i, 2 * lev + x], "expert", partner)

    def spread(i, lev, src):
        @pl.when((lev <= z) & (z < 3))
        def _():
            ups(i, lev, src).start()

        @pl.when((lev >= z) & (z > 0))
        def _():
            downs(i, lev, src).start()

        crosses(i, lev, src).start()

    def arrived(i, blk):
        send(xg.at[i, blk], xg.at[i, blk], x_sent.at[i, 0], got.at[i, blk], "expert", partner).wait_recv()

    def probs_to(other):
        return send(p_ref, p_all.at[me], p_sent.at[other], p_got.at[me], "expert", other)

    def probs_from(blk):
        send(p_ref, p_all.at[blk], p_sent.at[0], p_got.at[blk], "expert", partner).wait_recv()

    def return_to(side, blk, h, to):
        at = pl.ds(h * half, half)
        return send(
            rows.at[blk, at], rin.at[side, blk, at], r_sent.at[h, blk], r_got.at[h, side, blk], "expert", to
        )

    def return_down(blk, h):
        return return_to(0, blk, h, me - 2)

    def return_up(blk, h):
        return return_to(1, blk, h, me + 2)

    def return_cross(blk, h):
        at = pl.ds(h * half, half)
        return send(rows.at[blk, at], xin.at[at], r_sent.at[h, blk], xin_got.at[h], "expert", partner)

    def pass_on(lev, blk, h):
        @pl.when(lev < z)
        def _():
            return_down(blk, h).start()

        @pl.when(lev > z)
        def _():
            return_up(blk, h).start()

    def add_in(side, blk, h):
        return_to(side, blk, h, partner).wait_recv()
        at = slice(h * half, (h + 1) * half)
        rows[blk, at] = (
            rows[blk, at].astype(jnp.float32) + rin[side, blk, at].astype(jnp.float32)
        ).astype(jnp.bfloat16)

    def relay(k, other):
        lev = level(k)
        blk = 2 * lev + lax.rem(x + other, 2)

        for h in range(2):
            @pl.when(lev < z)
            def _():
                add_in(0, blk, h)

            @pl.when(lev > z)
            def _():
                add_in(1, blk, h)

            pass_on(lev, blk, h)

    def finish(blk, h):
        @pl.when(z < 3)
        def _():
            add_in(0, blk, h)

        @pl.when(z > 0)
        def _():
            add_in(1, blk, h)

    loads = [
        pltpu.make_async_copy(src, dst, loaded.at[i])
        for i, (src, dst) in enumerate(
            ((x_hbm, xg.at[0, me]), (g_hbm, xg.at[1, me]), (w_hbm, w_ref), (dn_hbm, dn_ref))
        )
    ]
    for load in loads:
        load.start()

    barrier = pltpu.get_barrier_semaphore()
    for step in range(1, 8):
        pl.semaphore_signal(
            barrier, inc=1, device_id={"expert": lax.rem(me + step, 8)}, device_id_type=pl.DeviceIdType.MESH
        )
    for to in (mate, across):
        pl.semaphore_signal(barrier, inc=1, device_id={"dp": to}, device_id_type=pl.DeviceIdType.MESH)
    pl.semaphore_wait(barrier, 9)

    for i in range(2):
        loads[i].wait()
        spread(i, z, xg.at[i, me])
    for step in range(1, 8):
        probs_to(lax.rem(me + step, 8)).start()
    p_all[me] = p_ref[...]
    acc[...] = jnp.zeros_like(acc)
    loads[2].wait()
    loads[3].wait()

    def work(blk):
        row_id = lax.broadcasted_iota(jnp.int32, (8, 128), 0)
        p_row = jnp.sum(jnp.where(row_id == me, p_all[blk], 0.0), axis=0, keepdims=True)
        p_cols = jnp.transpose(jnp.broadcast_to(p_row, (128, 128)))
        p_wide = jnp.concatenate([p_cols] * (ff // 128), axis=1)
        projected = jnp.dot(xg[0, blk], w_ref[...], preferred_element_type=jnp.float32)
        grad_hidden = jnp.dot(xg[1, blk], dn_ref[...], preferred_element_type=jnp.float32) * p_wide
        gate_pre = projected[:, :ff]
        up_part = projected[:, ff:]
        s = jax.nn.sigmoid(gate_pre)
        activated = gate_pre * s
        hp[blk] = (activated * up_part * p_wide).astype(jnp.bfloat16)
        gp[blk, :, :ff] = (grad_hidden * up_part * s * (1.0 + gate_pre * (1.0 - s))).astype(jnp.bfloat16)
        gp[blk, :, ff:] = (grad_hidden * activated).astype(jnp.bfloat16)
        rows[blk] = lax.dot_general(
            gp[blk], w_ref[...], (((1,), (1,)), ((), ())), preferred_element_type=jnp.float32
        ).astype(jnp.bfloat16)

    def relay_block(k):
        ahead = level(k)
        for i in range(2):
            arrived(i, 2 * ahead + x)
            spread(i, ahead, xg.at[i, 2 * ahead + x])

    def weights(lev, last):
        pair = pl.ds(2 * lev, 2)
        gp_two = gp[pair].reshape(256, 2 * ff)
        hp_two = hp[pair].reshape(256, ff)
        for q in range(4):
            at = slice(q * quarter, (q + 1) * quarter)
            for i, right, cols in ((0, gp_two, slice(0, 2 * ff)), (1, hp_two, slice(2 * ff, 3 * ff))):
                term = acc[at, cols] + lax.dot_general(
                    xg[i, pair, :, at].reshape(256, quarter), right,
                    (((0,), (0,)), ((), ())), preferred_element_type=jnp.float32,
                )
                if last:
                    part[q, :, cols] = term.astype(jnp.bfloat16)
                else:
                    acc[at, cols] = term

    def step(s, carry):
        k, other = s // 2, lax.rem(s, 2)
        lev = level(k)
        blk = 2 * lev + lax.rem(x + other, 2)

        @pl.when((other == 1) & (k + middle < 3))
        def _():
            relay_block(k + 1 + middle * ((k + 1) // 2))

        @pl.when((s == 1) & (middle == 1))
        def _():
            relay_block(2)

        @pl.when((s == 7) & (middle == 1))
        def _():
            relay(2, 0)
            relay(3, 0)

        @pl.when(other == 1)
        def _():
            for i in range(2):
                arrived(i, blk)

        @pl.when(s > 0)
        def _():
            probs_from(blk)

        work(blk)

        @pl.when((middle == 0) & (k > 0))
        def _():
            pass_on(lev, blk, 0)
            pass_on(lev, blk, 1)

        @pl.when((other == 1) & (k < 3))
        def _():
            weights(lev, False)

        return carry

    lax.fori_loop(0, 8, step, 0)

    weights(level(3), True)

    def to_mate(i, row):
        return send(part.at[row], mate_in.at[i], dp_sent.at[i], dp_got.at[i], "dp", mate)

    first = to_mate(0, 2 * (1 - y) + (1 - core))
    second = to_mate(1, mate)
    first.start()
    second.start()

    @pl.when(middle == 1)
    def _():
        relay(2, 1)
        relay(1, 0)

    first.wait_recv()
    y_sum[...] = (part[across].astype(jnp.float32) + mate_in[0].astype(jnp.float32)).astype(jnp.bfloat16)
    over = send(y_sum, y_in, dp_sent.at[2], dp_got.at[2], "dp", across)
    over.start()

    @pl.when(middle == 1)
    def _():
        relay(3, 1)
        relay(1, 1)

    for h in range(2):
        finish(partner, h)
        return_cross(partner, h).start()
    for h in range(2):
        finish(me, h)

    second.wait_recv()
    over.wait_recv()
    total = part[dp].astype(jnp.float32) + mate_in[1].astype(jnp.float32) + y_in[...].astype(jnp.float32)
    ggu_ref[...] = total[:, : 2 * ff]
    gd_ref[...] = total[:, 2 * ff :]

    for h in range(2):
        return_cross(partner, h).wait_recv()
    gi_ref[...] = (rows[me].astype(jnp.float32) + xin[...].astype(jnp.float32)).astype(jnp.bfloat16)

    first.wait_send()
    second.wait_send()
    over.wait_send()
    for h in range(2):
        return_cross(partner, h).wait_send()
    for i in range(7):
        probs_to(lax.rem(me + 1 + i, 8)).wait_send()
    for lev in range(4):
        for i in range(2):
            src = xg.at[i, 2 * lev + x]

            @pl.when((lev <= z) & (z < 3))
            def _():
                ups(i, lev, src).wait_send()

            @pl.when((lev >= z) & (z > 0))
            def _():
                downs(i, lev, src).wait_send()

            crosses(i, lev, src).wait_send()
            blk = 2 * lev + i

            @pl.when(lev < z)
            def _():
                return_down(blk, 0).wait_send()
                return_down(blk, 1).wait_send()

            @pl.when(lev > z)
            def _():
                return_up(blk, 0).wait_send()
                return_up(blk, 1).wait_send()


def dense_device(x_in, grad_out, routes, gate_probs, gate_up, down):
    owners = lax.axis_size("expert")
    tokens, width = x_in.shape
    hidden_units = down.shape[2]
    cols = 3 * hidden_units
    quarter = width // 4
    ids = jnp.arange(owners, dtype=jnp.int32)
    prob_by_expert = jnp.sum(
        jnp.where(routes.T[:, None, :] == ids[None, :, None], gate_probs.T[:, None, :], 0.0), axis=0
    )
    bf16, f32, dma = jnp.bfloat16, jnp.float32, pltpu.SemaphoreType.DMA
    vmem = pl.BlockSpec(memory_space=pltpu.VMEM)
    grad_in, grad_gate_up, grad_down = pl.pallas_call(
        fused_kernel,
        out_shape=(
            jax.ShapeDtypeStruct((tokens, width), bf16),
            jax.ShapeDtypeStruct((quarter, 2 * hidden_units), f32),
            jax.ShapeDtypeStruct((quarter, hidden_units), f32),
        ),
        in_specs=[vmem] + [pl.BlockSpec(memory_space=pl.ANY)] * 4,
        out_specs=(vmem,) * 3,
        scratch_shapes=[
            pltpu.VMEM((width, 2 * hidden_units), bf16),
            pltpu.VMEM((width, hidden_units), bf16),
            pltpu.VMEM((2, owners, tokens, width), bf16),
            pltpu.VMEM((owners, owners, tokens), f32),
            pltpu.VMEM((owners, tokens, width), bf16),
            pltpu.VMEM((2, owners, tokens, width), bf16),
            pltpu.VMEM((tokens, width), bf16),
            pltpu.VMEM((owners, tokens, 2 * hidden_units), bf16),
            pltpu.VMEM((owners, tokens, hidden_units), bf16),
            pltpu.VMEM((width, cols), f32),
            pltpu.VMEM((4, quarter, cols), bf16),
            pltpu.VMEM((2, quarter, cols), bf16),
            pltpu.VMEM((quarter, cols), bf16),
            pltpu.VMEM((quarter, cols), bf16),
            dma((2, owners)),
            dma((2, 4)),
            dma((2, 4)),
            dma((2, 4)),
            dma((owners,)),
            dma((owners,)),
            dma((2, 2, owners)),
            dma((2, owners)),
            dma((2,)),
            dma((3,)),
            dma((3,)),
            dma((4,)),
        ],
        compiler_params=pltpu.CompilerParams(
            collective_id=0, has_side_effects=True, vmem_limit_bytes=50 * 1024 * 1024
        ),
    )(prob_by_expert, x_in, grad_out, gate_up[0], down[0])
    return (grad_in, grad_gate_up[None], grad_down[None])


def per_device(x_in, grad_out, routes, gate_probs, gate_up, down):
    lines = (lax.axis_size("expert"), lax.axis_size("dp"), routes.shape[1], x_in.shape[0])
    if lines == (8, 4, 8, 128):
        return dense_device(x_in, grad_out, routes, gate_probs, gate_up, down)
    owners = lax.axis_size("expert")
    tokens_here = x_in.shape[0]
    top_count = routes.shape[1]
    width = x_in.shape[1]
    capacity = min(tokens_here, tokens_here * top_count * 9 // (8 * owners))
    slot_table, entry_pos = dispatch_table(routes, owners, capacity)
    sent_rows, sent_grads = send_rows(x_in, grad_out, gate_probs, slot_table, top_count)
    sent_rows = sent_rows.reshape(owners, capacity, width)
    sent_grads = sent_grads.reshape(owners, capacity, width)
    proj_weight = gate_up[0]
    down_weight = down[0]
    recv_rows, recv_grads = (
        lax.all_to_all(sent_rows, "expert", split_axis=0, concat_axis=0, tiled=True),
        lax.all_to_all(sent_grads, "expert", split_axis=0, concat_axis=0, tiled=True),
    )
    rows_in = recv_rows.reshape(-1, width)
    scaled = recv_grads.reshape(-1, width)
    grad_rows, grad_proj, hidden = expert_rows(rows_in, scaled, proj_weight, down_weight)
    returned = lax.all_to_all(
        grad_rows.reshape(owners, capacity, width),
        "expert",
        split_axis=0,
        concat_axis=0,
        tiled=True,
    )
    hidden_units = hidden.shape[1]
    grad_term = weight_terms(rows_in, scaled, grad_proj, hidden)
    grad_share = lax.psum_scatter(
        grad_term.astype(jnp.bfloat16), "dp", scatter_dimension=0, tiled=True
    ).astype(jnp.float32)
    grad_gate_up = grad_share[None, :, : 2 * hidden_units]
    grad_down = grad_share[None, :, 2 * hidden_units :]
    entries = returned.reshape(-1, width)[entry_pos]
    grad_in = jnp.sum(
        entries.reshape(tokens_here, top_count, width).astype(jnp.float32), axis=1
    ).astype(jnp.bfloat16)
    return (grad_in, grad_gate_up, grad_down)


def solution(mesh):
    placed = (
        P(("dp", "expert"), None),
        P(("dp", "expert"), None),
        P(("dp", "expert"), None),
        P(("dp", "expert"), None),
        P("expert", None, None),
        P("expert", None, None),
    )
    return jax.shard_map(
        per_device,
        mesh=mesh,
        in_specs=placed,
        out_specs=(P(("dp", "expert"), None), P("expert", "dp", None), P("expert", "dp", None)),
        check_vma=False,
    )
```
